1024 devices in a mesh: seq: 128 (over z, y, core), head: 8 (over x).
Axes of the slice: x: 8, y: 8, z: 8, core: 2. Of those that a mesh axis runs over, the one named last changes fastest.
Arguments:
- queries: bfloat16 [65536, 4096], P(('seq', 'head')), may hold values from -6 to 6
- keys_in: bfloat16 [65536, 4096], P(('seq', 'head')), may hold values from -6 to 6
- values_in: bfloat16 [65536, 4096], P(('seq', 'head')), may hold values from -8 to 8, as said below
- gain: float32 [4096], replicated, may hold values from 0.1 to 1.9
Outputs:
- normed: bfloat16 [65536, 4096], P(('seq', 'head'))
The draws below stay inside these ranges and needn't reach their ends.
Inputs may be any that keep to these rules, and one draw needn't show every extreme that they name: `values_in`: values of order one whose typical size differs from column to column.
All inputs are finite; a program needn't handle non-finite values.
Results may differ from the reference program's by a relative error of at most 0.0058.
Values may be sent and summed in bfloat16 or wider, within the bound.
A program may use at most 128 MiB of HBM per device.

```python
import math
import jax
import jax.numpy as jnp
from jax import lax

H = 32
HD = 128
D = 4096
TOK_DEV = 64
TOKENS = 65536
N_SEQ = 128
N_HEAD = 8


def draw_values_in(key, part):
    first, second = jax.random.split(key, 2)
    column_scale = jnp.exp(jax.random.uniform(first, (D,), jnp.float32, math.log(0.3), math.log(3.0)))
    base = jax.random.normal(second, (TOKENS, D), jnp.float32)
    return jnp.clip(base * column_scale[None, :], -8.0, 8.0).astype(jnp.bfloat16)


def levels(key, shape, cuts, smallest, high):
    def one(dim, shards_of):
        heights = jax.random.uniform(jax.random.fold_in(jax.random.fold_in(key, 6), dim), (shards_of,), jnp.float32, smallest / len(cuts), high / len(cuts))
        return jnp.repeat(jnp.exp(heights), shape[dim] // shards_of).reshape((-1,) + (1,) * (len(shape) - dim - 1))

    level = one(*cuts[0])
    for cut in cuts[1:]:
        level = level * one(*cut)
    return level


def scatter_about(key, extent, scale, bound, shards=(), kind=jnp.bfloat16):
    level = levels(key, extent, shards, -0.22, 0.18) if shards else 1.0
    values = jax.random.normal(key, extent, jnp.float32) * scale * level
    return jnp.minimum(jnp.maximum(values, -bound), bound).astype(kind)


def setup_inputs(seed: int = 0) -> dict:
    key_of = jax.random.split(jax.random.key(seed), 5)
    return {
        "queries": scatter_about(key_of[0], (TOKENS, D), 1.0, 6.0, ((0, 1024),)),
        "keys_in": scatter_about(key_of[1], (TOKENS, D), 1.0, 6.0, ((0, 1024),)),
        "values_in": draw_values_in(jax.random.fold_in(key_of[4], 71), 0),
        "gain": jnp.clip(1.0 + 0.18 * jax.random.normal(key_of[3], (D,), jnp.float32), 0.1, 1.9),
    }


def reference(queries, keys_in, values_in, gain):
    shard_len = TOK_DEV * N_HEAD
    blocks = N_SEQ
    q_act = jax.nn.silu(queries.astype(jnp.float32)).astype(jnp.bfloat16).reshape(blocks, shard_len, H, HD)
    k_act = jax.nn.silu(keys_in.astype(jnp.float32)).astype(jnp.bfloat16).reshape(blocks, shard_len, H, HD)
    values = values_in.reshape(blocks, shard_len, H, HD)
    causal_mask = jnp.tril(jnp.ones((shard_len, shard_len), dtype=bool))

    def advance(carry_state, pieces):
        q_blk, k_blk, v_blk = pieces
        scores = jnp.einsum('thd,shd->hts', q_blk.astype(jnp.float32), k_blk.astype(jnp.float32))
        weights = jnp.where(causal_mask[None], scores, 0.0).astype(jnp.bfloat16)
        intra = jnp.einsum('hts,shd->thd', weights.astype(jnp.float32), v_blk.astype(jnp.float32))
        prefix = carry_state.astype(jnp.bfloat16)
        inter = jnp.einsum('thd,hde->the', q_blk.astype(jnp.float32), prefix.astype(jnp.float32))
        local_state = jnp.einsum('shd,she->hde', k_blk.astype(jnp.float32), v_blk.astype(jnp.float32))
        attn = (intra + inter).astype(jnp.bfloat16)
        return (carry_state + local_state, attn)
    start_state = jnp.zeros((H, HD, HD), jnp.float32)
    _, attn = lax.scan(advance, start_state, (q_act, k_act, values))
    widened = attn.reshape(TOKENS, D).astype(jnp.float32)
    mean_square = lax.optimization_barrier(jnp.mean(widened * widened, axis=-1, keepdims=True))
    return (widened * lax.rsqrt(mean_square + 1e-05) * gain[None, :]).astype(jnp.bfloat16)
```

```python
import functools

import jax
import jax.numpy as jnp
from jax import lax
from jax.experimental import pallas as pl
from jax.experimental.pallas import tpu as pltpu
from jax.sharding import PartitionSpec as P

HD = 128
GROUP = 16
MESH = pl.DeviceIdType.MESH
BF16, F32 = jnp.bfloat16, jnp.float32


def silu(x):
    wide = x.astype(F32)
    return (wide / (1.0 + jnp.exp(-wide))).astype(BF16)


def far_first(n):
    return sorted(range(1, n), key=lambda d: -min(d, n - d))


def kernel(nx, nz, q_hbm, k_hbm, v_hbm, gain_ref, out_ref, q_raw, k_raw, kv, q_act, kv_in, q_in, t_buf, r1, r_sum, r2,
           p_out, p_in, acc, o_buf, a_in, in_sem, kv_s, kv_r, q_s, q_r, r1_s, r1_r, r2_s, r2_r, r3_s, r3_r, o_s, o_r,
           late):
    x, s = lax.axis_index("head"), lax.axis_index("seq")
    g, z = lax.rem(s, GROUP), s // GROUP
    rows = q_raw.shape[0]
    width = kv_in.shape[-1]
    heads = width // HD
    toks = nx * rows
    piece = t_buf.shape[1] // GROUP

    def at_x(t):
        return {"head": t}

    def at_g(t):
        return {"seq": z * GROUP + t}

    def at_z(t):
        return {"seq": t * GROUP + g}

    first = (x == 0) & (s == 0)
    line_first = (s == 0) & (x != 0)
    plane_first = (x == 0) & (z == 0) & (g != 0)
    stack_first = (x == 0) & (g == 0) & (z != 0)

    loads = [
        pltpu.make_async_copy(k_hbm, k_raw, in_sem.at[0]),
        pltpu.make_async_copy(v_hbm, kv.at[1], in_sem.at[1]),
        pltpu.make_async_copy(q_hbm, q_raw, in_sem.at[2]),
    ]
    for load in loads:
        load.start()

    barrier = pltpu.get_barrier_semaphore()
    peers = ((nx, x, at_x), (GROUP, g, at_g), (nz, z, at_z))
    n_peers = sum(n - 1 for n, _, _ in peers)

    def greet(sem):
        for n, me, at in peers:
            for d in range(1, n):
                pl.semaphore_signal(sem, inc=1, device_id=at(lax.rem(me + d, n)), device_id_type=MESH)

    @pl.when(jnp.logical_not(first))
    def _():
        greet(barrier)

    loads[0].wait()
    kv[0] = silu(k_raw[...])
    loads[1].wait()

    pl.semaphore_wait(barrier, n_peers - (line_first | plane_first | stack_first).astype(jnp.int32))

    @pl.when(first)
    def _():
        greet(late)

    def columns(t, half):
        return pl.ds(pl.multiple_of(t * 2 * width + half * width, width), width)

    def kv_copy(t, half):
        return kv.at[:, :, columns(t, half)], kv_in.at[half, x], kv_s.at[half], kv_r.at[half]

    def q_copy(t, half):
        return q_act.at[:, columns(t, half)], q_in.at[half, x], q_s.at[half], q_r.at[half]

    def remote(copy, device):
        src, dst, send, recv = copy
        pltpu.make_async_remote_copy(src, dst, send, recv, device_id=device, device_id_type=MESH).start()

    def local(copy):
        src, dst, _, recv = copy
        pltpu.make_async_copy(src, dst, recv).start()

    def wait(ref, sem):
        pltpu.make_async_copy(ref, ref, sem).wait()

    def spread_x(copy_of, half, open_late):
        for d in far_first(nx):
            t = lax.rem(x + d, nx)
            if open_late:
                @pl.when(jnp.logical_not((s == 0) & (t == 0)))
                def _():
                    remote(copy_of(t, half), at_x(t))
            else:
                remote(copy_of(t, half), at_x(t))
        local(copy_of(x, half))

    spread_x(kv_copy, 0, True)
    spread_x(kv_copy, 1, True)
    loads[2].wait()
    q_act[...] = silu(q_raw[...])
    spread_x(q_copy, 0, True)
    spread_x(q_copy, 1, True)

    @pl.when(line_first | plane_first | stack_first)
    def _():
        pl.semaphore_wait(late, 1)

    @pl.when(line_first)
    def _():
        for half in range(2):
            remote(kv_copy(0, half), at_x(0))
        for half in range(2):
            remote(q_copy(0, half), at_x(0))

    def tokens(ref):
        return ref.reshape(toks, width)

    def state(half):
        wait(kv_in.at[half], kv_r.at[half])
        keys, vals = tokens(kv_in[half, :, 0]), tokens(kv_in[half, :, 1])
        for h in range(heads):
            cols = slice(h * HD, (h + 1) * HD)
            t_buf[half, cols, :] = lax.dot_general(
                keys[:, cols], vals[:, cols], (((0,), (0,)), ((), ())), preferred_element_type=F32
            )
        for d in range(GROUP):
            t = lax.rem(g + d, GROUP) if d else g
            span = pl.ds(pl.multiple_of(t * piece, piece), piece)
            copy = (t_buf.at[half, span], r1.at[half, g], r1_s.at[half], r1_r.at[half])
            if d:
                remote(copy, at_g(t))
            else:
                local(copy)

    def plane_sum(half):
        wait(r1.at[half], r1_r.at[half])
        r_sum[half] = jnp.sum(r1[half], axis=0)
        for d in range(nz):
            t = lax.rem(z + d, nz) if d else z
            copy = (r_sum.at[half], r2.at[half, z], r2_s.at[half], r2_r.at[half])
            if d:
                remote(copy, at_z(t))
            else:
                local(copy)

    def prefixes(half):
        wait(r2.at[half], r2_r.at[half])
        running = jnp.zeros(r_sum.shape[1:], F32)
        for i in range(nz):
            running = running + jnp.where(i < z, r2[half, i], 0.0)
        for j in range(GROUP):
            p_out[half, j] = running.astype(BF16)
            running = running + r1[half, j]
        for d in range(GROUP):
            t = lax.rem(g + d, GROUP) if d else g
            span = pl.ds(pl.multiple_of(g * piece, piece), piece)
            copy = (p_out.at[half, t], p_in.at[half, span], r3_s.at[half], r3_r.at[half])
            if d:
                remote(copy, at_g(t))
            else:
                local(copy)

    block = toks // 2
    causal = lax.broadcasted_iota(jnp.int32, (block, block), 1) <= lax.broadcasted_iota(jnp.int32, (block, block), 0)

    def weighted(queries, keys, vals, masked):
        scores = lax.dot_general(queries, keys, (((1,), (1,)), ((), ())), preferred_element_type=F32)
        if masked:
            scores = jnp.where(causal, scores, 0.0)
        return jnp.dot(scores.astype(BF16), vals, preferred_element_type=F32)

    def intra(half):
        wait(q_in.at[half], q_r.at[half])
        queries = tokens(q_in[half])
        keys, vals = tokens(kv_in[half, :, 0]), tokens(kv_in[half, :, 1])
        for h in range(heads):
            cols = slice(h * HD, (h + 1) * HD)
            q, k, v = queries[:, cols], keys[:, cols], vals[:, cols]
            acc[half, :block, cols] = weighted(q[:block], k[:block], v[:block], True)
            acc[half, block:, cols] = weighted(q[block:], k[block:], v[block:], True) + weighted(
                q[block:], k[:block], v[:block], False
            )

    def finish(half):
        wait(p_in.at[half], r3_r.at[half])
        queries = tokens(q_in[half])
        for h in range(heads):
            cols = slice(h * HD, (h + 1) * HD)
            inter = jnp.dot(queries[:, cols], p_in[half, cols, :], preferred_element_type=F32)
            o_buf[half, :, :, cols] = (acc[half, :, cols] + inter).astype(BF16).reshape(nx, rows, HD)

        def o_copy(t, half):
            return o_buf.at[half, t], a_in.at[:, columns(x, half)], o_s.at[half], o_r.at[half]

        spread_x(o_copy, half, False)

    state(0)
    plane_sum(0)
    state(1)
    prefixes(0)
    plane_sum(1)
    intra(0)
    finish(0)
    prefixes(1)
    intra(1)
    finish(1)

    for half in range(2):
        wait(a_in.at[:, pl.ds(0, nx * width)], o_r.at[half])
    wide = a_in[...].astype(F32)
    mean_square = jnp.mean(wide * wide, axis=-1, keepdims=True)
    out_ref[...] = (wide * lax.rsqrt(mean_square + 1e-05) * gain_ref[...]).astype(BF16)

    for half in range(2):
        wait(kv_in.at[half, pl.ds(0, nx - 1)], kv_s.at[half])
        wait(q_in.at[half, pl.ds(0, nx - 1)], q_s.at[half])
        wait(o_buf.at[half, pl.ds(0, nx - 1)], o_s.at[half])
        wait(r1.at[half, pl.ds(0, GROUP - 1)], r1_s.at[half])
        wait(r2.at[half, pl.ds(0, nz - 1)], r2_s.at[half])
        wait(p_out.at[half, pl.ds(0, GROUP - 1)], r3_s.at[half])


def solution(mesh):
    nx, nz = mesh.shape["head"], mesh.shape["seq"] // GROUP

    def local(queries, keys_in, values_in, gain):
        rows, d = queries.shape
        width = d // nx // 2
        piece = width // GROUP
        vmem, pair = pltpu.VMEM, pltpu.SemaphoreType.DMA((2,))
        return pl.pallas_call(
            functools.partial(kernel, nx, nz),
            out_shape=jax.ShapeDtypeStruct((rows, d), BF16),
            in_specs=[pl.BlockSpec(memory_space=pl.ANY)] * 3 + [pl.BlockSpec(memory_space=pltpu.VMEM)],
            out_specs=pl.BlockSpec(memory_space=pltpu.VMEM),
            scratch_shapes=[
                vmem((rows, d), BF16),
                vmem((rows, d), BF16),
                vmem((2, rows, d), BF16),
                vmem((rows, d), BF16),
                vmem((2, nx, 2, rows, width), BF16),
                vmem((2, nx, rows, width), BF16),
                vmem((2, width, HD), F32),
                vmem((2, GROUP, piece, HD), F32),
                vmem((2, piece, HD), F32),
                vmem((2, nz, piece, HD), F32),
                vmem((2, GROUP, piece, HD), BF16),
                vmem((2, width, HD), BF16),
                vmem((2, nx * rows, width), F32),
                vmem((2, nx, rows, width), BF16),
                vmem((rows, d), BF16),
                pltpu.SemaphoreType.DMA((3,)),
            ]
            + [pair] * 12
            + [pltpu.SemaphoreType.REGULAR],
            compiler_params=pltpu.CompilerParams(
                collective_id=0, has_side_effects=True, vmem_limit_bytes=40 * 2**20
            ),
        )(queries, keys_in, values_in, gain.reshape(1, d))

    placed = P(("seq", "head"), None)
    return jax.shard_map(
        local, mesh=mesh, in_specs=(placed, placed, placed, P()), out_specs=placed, check_vma=False
    )
```

```python
import functools

import jax
import jax.numpy as jnp
from jax import lax
from jax.experimental import pallas as pl
from jax.experimental.pallas import tpu as pltpu
from jax.sharding import PartitionSpec as P

HD = 128
GROUP = 16
MESH = pl.DeviceIdType.MESH
BF16, F32 = jnp.bfloat16, jnp.float32


def silu(x):
    wide = x.astype(F32)
    return (wide / (1.0 + jnp.exp(-wide))).astype(BF16)


def far_first(n):
    return sorted(range(1, n), key=lambda d: -min(d, n - d))


def kernel(nx, nz, q_hbm, k_hbm, v_hbm, attn, scale, q_raw, k_raw, kv, q_act, kv_in, q_in, t_buf, r1, r_sum, r2,
           below, p_out, p_in, acc, o_buf, in_sem, kv_s, kv_r, q_s, q_r, r1_s, r1_r, r2_s, r2_r, r3_s, r3_r, o_s, o_r,
           late, above):
    x, s = lax.axis_index("head"), lax.axis_index("seq")
    g, z = lax.rem(s, GROUP), s // GROUP
    rows = q_raw.shape[0]
    width = kv_in.shape[-1]
    heads = width // HD
    toks = nx * rows
    piece = t_buf.shape[1] // GROUP

    def at_x(t):
        return {"head": t}

    def at_g(t):
        return {"seq": z * GROUP + t}

    def at_z(t):
        return {"seq": t * GROUP + g}

    first = (x == 0) & (s == 0)
    line_first = (s == 0) & (x != 0)
    plane_first = (x == 0) & (z == 0) & (g != 0)

    loads = [
        pltpu.make_async_copy(k_hbm, k_raw, in_sem.at[0]),
        pltpu.make_async_copy(v_hbm, kv.at[1], in_sem.at[1]),
        pltpu.make_async_copy(q_hbm, q_raw, in_sem.at[2]),
    ]
    for load in loads:
        load.start()

    barrier = pltpu.get_barrier_semaphore()
    peers = ((nx, x, at_x), (GROUP, g, at_g))

    def greet(sem):
        for n, me, at in peers:
            for d in range(1, n):
                pl.semaphore_signal(sem, inc=1, device_id=at(lax.rem(me + d, n)), device_id_type=MESH)

    @pl.when(jnp.logical_not(first))
    def _():
        greet(barrier)

    for i in range(1, nz):
        @pl.when(i > z)
        def _():
            pl.semaphore_signal(barrier, inc=1, device_id=at_z(i), device_id_type=MESH)

    loads[0].wait()
    kv[0] = silu(k_raw[...])
    loads[1].wait()

    pl.semaphore_wait(barrier, nx + GROUP - 2 + z - (line_first | plane_first).astype(jnp.int32))

    @pl.when(first)
    def _():
        greet(late)

    for i in range(nz - 1):
        @pl.when(i < z)
        def _():
            pl.semaphore_signal(above, inc=1, device_id=at_z(i), device_id_type=MESH)

    def columns(t, half):
        return pl.ds(pl.multiple_of(t * 2 * width + half * width, width), width)

    def kv_copy(t, half):
        return kv.at[:, :, columns(t, half)], kv_in.at[half, x], kv_s.at[half], kv_r.at[half]

    def q_copy(t, half):
        return q_act.at[:, columns(t, half)], q_in.at[half, x], q_s.at[half], q_r.at[half]

    def remote(copy, device):
        src, dst, send, recv = copy
        pltpu.make_async_remote_copy(src, dst, send, recv, device_id=device, device_id_type=MESH).start()

    def local(copy):
        src, dst, _, recv = copy
        pltpu.make_async_copy(src, dst, recv).start()

    def wait(ref, sem):
        pltpu.make_async_copy(ref, ref, sem).wait()

    def spread_x(copy_of, half, open_late):
        for d in far_first(nx):
            t = lax.rem(x + d, nx)
            if open_late:
                @pl.when(jnp.logical_not((s == 0) & (t == 0)))
                def _():
                    remote(copy_of(t, half), at_x(t))
            else:
                remote(copy_of(t, half), at_x(t))
        local(copy_of(x, half))

    spread_x(kv_copy, 0, True)
    loads[2].wait()
    q_act[...] = silu(q_raw[...])

    @pl.when(line_first | plane_first)
    def _():
        pl.semaphore_wait(late, 1)

    @pl.when(line_first)
    def _():
        remote(kv_copy(0, 0), at_x(0))

    spread_x(kv_copy, 1, False)
    spread_x(q_copy, 0, False)
    spread_x(q_copy, 1, False)

    def tokens(ref):
        return ref.reshape(toks, width)

    def state(half):
        wait(kv_in.at[half], kv_r.at[half])
        keys, vals = tokens(kv_in[half, :, 0]), tokens(kv_in[half, :, 1])
        for h in range(heads):
            cols = slice(h * HD, (h + 1) * HD)
            t_buf[half, cols, :] = lax.dot_general(
                keys[:, cols], vals[:, cols], (((0,), (0,)), ((), ())), preferred_element_type=F32
            )
        for d in range(GROUP):
            t = lax.rem(g + d, GROUP) if d else g
            span = pl.ds(pl.multiple_of(t * piece, piece), piece)
            copy = (t_buf.at[half, span], r1.at[half, g], r1_s.at[half], r1_r.at[half])
            if d:
                remote(copy, at_g(t))
            else:
                local(copy)

    def plane_sum(half):
        wait(r1.at[half], r1_r.at[half])
        r_sum[half] = jnp.sum(r1[half], axis=0)
        if half == 0:
            @pl.when(z < nz - 1)
            def _():
                pl.semaphore_wait(above, nz - 1 - z)

        for i in range(1, nz):
            @pl.when(i > z)
            def _():
                remote((r_sum.at[half], r2.at[half, z], r2_s.at[half, i], r2_r.at[half, z]), at_z(i))

    def prefixes(half):
        below[half] = jnp.zeros(r_sum.shape[1:], F32)
        for i in range(nz - 1):
            @pl.when(i < z)
            def _():
                wait(r2.at[half, i], r2_r.at[half, i])
                below[half] += r2[half, i]
        running = below[half]
        for j in range(GROUP):
            p_out[half, j] = running.astype(BF16)
            running = running + r1[half, j]
        for d in range(GROUP):
            t = lax.rem(g + d, GROUP) if d else g
            span = pl.ds(pl.multiple_of(g * piece, piece), piece)
            copy = (p_out.at[half, t], p_in.at[half, span], r3_s.at[half], r3_r.at[half])
            if d:
                remote(copy, at_g(t))
            else:
                local(copy)

    block = toks // 2
    causal = lax.broadcasted_iota(jnp.int32, (block, block), 1) <= lax.broadcasted_iota(jnp.int32, (block, block), 0)

    def weighted(queries, keys, vals, masked):
        scores = lax.dot_general(queries, keys, (((1,), (1,)), ((), ())), preferred_element_type=F32)
        if masked:
            scores = jnp.where(causal, scores, 0.0)
        return jnp.dot(scores.astype(BF16), vals, preferred_element_type=F32)

    def intra(half):
        wait(q_in.at[half], q_r.at[half])
        queries = tokens(q_in[half])
        keys, vals = tokens(kv_in[half, :, 0]), tokens(kv_in[half, :, 1])
        for h in range(heads):
            cols = slice(h * HD, (h + 1) * HD)
            q, k, v = queries[:, cols], keys[:, cols], vals[:, cols]
            acc[half, :block, cols] = weighted(q[:block], k[:block], v[:block], True)
            acc[half, block:, cols] = weighted(q[block:], k[block:], v[block:], True) + weighted(
                q[block:], k[:block], v[:block], False
            )

    def finish(half):
        wait(p_in.at[half], r3_r.at[half])
        queries = tokens(q_in[half])
        for h in range(heads):
            cols = slice(h * HD, (h + 1) * HD)
            inter = jnp.dot(queries[:, cols], p_in[half, cols, :], preferred_element_type=F32)
            o_buf[half, :, :, cols] = (acc[half, :, cols] + inter).astype(BF16).reshape(nx, rows, HD)

        def o_copy(t, half):
            return o_buf.at[half, t], attn.at[:, columns(x, half)], o_s.at[half], o_r.at[half]

        spread_x(o_copy, half, False)

    state(0)
    plane_sum(0)
    state(1)
    prefixes(0)
    plane_sum(1)
    intra(0)
    finish(0)
    prefixes(1)
    intra(1)
    finish(1)

    for half in range(2):
        wait(attn.at[:, pl.ds(0, nx * width)], o_r.at[half])
    wide = attn[...].astype(F32)
    scale[...] = lax.rsqrt(jnp.mean(wide * wide, axis=-1, keepdims=True) + 1e-05)

    for half in range(2):
        wait(kv_in.at[half, pl.ds(0, nx - 1)], kv_s.at[half])
        wait(q_in.at[half, pl.ds(0, nx - 1)], q_s.at[half])
        wait(o_buf.at[half, pl.ds(0, nx - 1)], o_s.at[half])
        wait(r1.at[half, pl.ds(0, GROUP - 1)], r1_s.at[half])
        wait(p_out.at[half, pl.ds(0, GROUP - 1)], r3_s.at[half])
        for i in range(1, nz):
            @pl.when(i > z)
            def _():
                wait(r_sum.at[half], r2_s.at[half, i])


def solution(mesh):
    nx, nz = mesh.shape["head"], mesh.shape["seq"] // GROUP

    def local(queries, keys_in, values_in, gain):
        rows, d = queries.shape
        width = d // nx // 2
        piece = width // GROUP
        vmem, pair = pltpu.VMEM, pltpu.SemaphoreType.DMA((2,))
        attn, scale = pl.pallas_call(
            functools.partial(kernel, nx, nz),
            out_shape=(jax.ShapeDtypeStruct((rows, d), BF16), jax.ShapeDtypeStruct((rows, 1), F32)),
            in_specs=[pl.BlockSpec(memory_space=pltpu.HBM)] * 3,
            out_specs=(pl.BlockSpec(memory_space=pltpu.VMEM),) * 2,
            scratch_shapes=[
                vmem((rows, d), BF16),
                vmem((rows, d), BF16),
                vmem((2, rows, d), BF16),
                vmem((rows, d), BF16),
                vmem((2, nx, 2, rows, width), BF16),
                vmem((2, nx, rows, width), BF16),
                vmem((2, width, HD), F32),
                vmem((2, GROUP, piece, HD), F32),
                vmem((2, piece, HD), F32),
                vmem((2, nz, piece, HD), F32),
                vmem((2, piece, HD), F32),
                vmem((2, GROUP, piece, HD), BF16),
                vmem((2, width, HD), BF16),
                vmem((2, nx * rows, width), F32),
                vmem((2, nx, rows, width), BF16),
                pltpu.SemaphoreType.DMA((3,)),
            ]
            + [pair] * 6
            + [pltpu.SemaphoreType.DMA((2, nz))] * 2
            + [pair] * 4
            + [pltpu.SemaphoreType.REGULAR] * 2,
            compiler_params=pltpu.CompilerParams(
                collective_id=0, has_side_effects=True, vmem_limit_bytes=55836672
            ),
        )(queries, keys_in, values_in)
        return (attn.astype(F32) * scale * gain[None, :]).astype(BF16)

    placed = P(("seq", "head"), None)
    return jax.shard_map(
        local, mesh=mesh, in_specs=(placed, placed, placed, P()), out_specs=placed, check_vma=False
    )
```

```python
import functools

import jax
import jax.numpy as jnp
from jax import lax
from jax.experimental import pallas as pl
from jax.experimental.pallas import tpu as pltpu
from jax.sharding import PartitionSpec as P

HD = 128
GROUP = 16
MESH = pl.DeviceIdType.MESH
BF16, F32 = jnp.bfloat16, jnp.float32


def silu(x):
    wide = x.astype(F32)
    return (wide / (1.0 + jnp.exp(-wide))).astype(BF16)


def far_first(n):
    return sorted(range(1, n), key=lambda d: -min(d, n - d))


def kernel(nx, nz, q_hbm, k_hbm, v_hbm, attn, scale, q_raw, k_raw, k_act, q_act, v_in, k_in, q_in, t_buf, r1, r_sum, r2,
           below, p_out, p_in, acc, o_buf, in_sem, v_s, v_r, k_s, k_r, q_s, q_r, r1_s, r1_r, r2_s, r2_r, r3_s, r3_r, o_s, o_r,
           late, above):
    x, s = lax.axis_index("head"), lax.axis_index("seq")
    g, z = lax.rem(s, GROUP), s // GROUP
    rows = q_raw.shape[0]
    width = k_in.shape[-1]
    heads = width // HD
    toks = nx * rows
    piece = t_buf.shape[1] // GROUP

    def at_x(t):
        return {"head": t}

    def at_g(t):
        return {"seq": z * GROUP + t}

    def at_z(t):
        return {"seq": t * GROUP + g}

    first = (x == 0) & (s == 0)
    line_first = (s == 0) & (x != 0)
    plane_first = (x == 0) & (z == 0) & (g != 0)

    loads = [
        pltpu.make_async_copy(k_hbm, k_raw, in_sem.at[0]),
        pltpu.make_async_copy(q_hbm, q_raw, in_sem.at[1]),
    ]
    for load in loads:
        load.start()

    barrier = pltpu.get_barrier_semaphore()
    peers = ((nx, x, at_x), (GROUP, g, at_g))

    def greet(sem):
        for n, me, at in peers:
            for d in range(1, n):
                pl.semaphore_signal(sem, inc=1, device_id=at(lax.rem(me + d, n)), device_id_type=MESH)

    @pl.when(jnp.logical_not(first))
    def _():
        greet(barrier)

    for i in range(1, nz):
        @pl.when(i > z)
        def _():
            pl.semaphore_signal(barrier, inc=1, device_id=at_z(i), device_id_type=MESH)

    pl.semaphore_wait(barrier, nx + GROUP - 2 + z - (line_first | plane_first).astype(jnp.int32))

    @pl.when(first)
    def _():
        greet(late)

    for i in range(nz - 1):
        @pl.when(i < z)
        def _():
            pl.semaphore_signal(above, inc=1, device_id=at_z(i), device_id_type=MESH)

    def columns(t, half):
        return pl.ds(pl.multiple_of(t * 2 * width + half * width, width), width)

    def v_copy(t, half):
        return v_hbm.at[:, columns(t, half)], v_in.at[half, x], v_s.at[half], v_r.at[half]

    def k_copy(t, half):
        return k_act.at[:, columns(t, half)], k_in.at[half, x], k_s.at[half], k_r.at[half]

    def q_copy(t, half):
        return q_act.at[:, columns(t, half)], q_in.at[half, x], q_s.at[half], q_r.at[half]

    def activate(raw, act, half):
        for t in range(nx):
            cols = slice((2 * t + half) * width, (2 * t + half + 1) * width)
            act[:, cols] = silu(raw[:, cols])

    def remote(copy, device):
        src, dst, send, recv = copy
        pltpu.make_async_remote_copy(src, dst, send, recv, device_id=device, device_id_type=MESH).start()

    def local(copy):
        src, dst, _, recv = copy
        pltpu.make_async_copy(src, dst, recv).start()

    def wait(ref, sem):
        pltpu.make_async_copy(ref, ref, sem).wait()

    def spread_x(copy_of, half, open_late):
        for d in far_first(nx):
            t = lax.rem(x + d, nx)
            if open_late:
                @pl.when(jnp.logical_not((s == 0) & (t == 0)))
                def _():
                    remote(copy_of(t, half), at_x(t))
            else:
                remote(copy_of(t, half), at_x(t))
        local(copy_of(x, half))

    spread_x(v_copy, 0, True)
    loads[0].wait()
    activate(k_raw, k_act, 0)
    spread_x(k_copy, 0, True)
    activate(k_raw, k_act, 1)

    @pl.when(line_first | plane_first)
    def _():
        pl.semaphore_wait(late, 1)

    @pl.when(line_first)
    def _():
        remote(v_copy(0, 0), at_x(0))
        remote(k_copy(0, 0), at_x(0))

    spread_x(v_copy, 1, False)
    spread_x(k_copy, 1, False)
    loads[1].wait()
    for half in range(2):
        activate(q_raw, q_act, half)
        spread_x(q_copy, half, False)

    def tokens(ref):
        return ref.reshape(toks, width)

    def state(half):
        wait(v_in.at[half], v_r.at[half])
        wait(k_in.at[half], k_r.at[half])
        keys, vals = tokens(k_in[half]), tokens(v_in[half])
        for h in range(heads):
            cols = slice(h * HD, (h + 1) * HD)
            t_buf[half, cols, :] = lax.dot_general(
                keys[:, cols], vals[:, cols], (((0,), (0,)), ((), ())), preferred_element_type=F32
            )
        for d in range(GROUP):
            t = lax.rem(g + d, GROUP) if d else g
            span = pl.ds(pl.multiple_of(t * piece, piece), piece)
            copy = (t_buf.at[half, span], r1.at[half, g], r1_s.at[half], r1_r.at[half])
            if d:
                remote(copy, at_g(t))
            else:
                local(copy)

    def plane_sum(half):
        wait(r1.at[half], r1_r.at[half])
        r_sum[half] = jnp.sum(r1[half], axis=0)
        if half == 0:
            @pl.when(z < nz - 1)
            def _():
                pl.semaphore_wait(above, nz - 1 - z)

        for i in range(1, nz):
            @pl.when(i > z)
            def _():
                remote((r_sum.at[half], r2.at[half, z], r2_s.at[half, i], r2_r.at[half, z]), at_z(i))

    def prefixes(half):
        below[half] = jnp.zeros(r_sum.shape[1:], F32)
        for i in range(nz - 1):
            @pl.when(i < z)
            def _():
                wait(r2.at[half, i], r2_r.at[half, i])
                below[half] += r2[half, i]
        running = below[half]
        for j in range(GROUP):
            p_out[half, j] = running.astype(BF16)
            running = running + r1[half, j]
        for d in range(GROUP):
            t = lax.rem(g + d, GROUP) if d else g
            span = pl.ds(pl.multiple_of(g * piece, piece), piece)
            copy = (p_out.at[half, t], p_in.at[half, span], r3_s.at[half], r3_r.at[half])
            if d:
                remote(copy, at_g(t))
            else:
                local(copy)

    block = toks // 2
    causal = lax.broadcasted_iota(jnp.int32, (block, block), 1) <= lax.broadcasted_iota(jnp.int32, (block, block), 0)

    def weighted(queries, keys, vals, masked):
        scores = lax.dot_general(queries, keys, (((1,), (1,)), ((), ())), preferred_element_type=F32)
        if masked:
            scores = jnp.where(causal, scores, 0.0)
        return jnp.dot(scores.astype(BF16), vals, preferred_element_type=F32)

    def intra(half):
        wait(q_in.at[half], q_r.at[half])
        queries = tokens(q_in[half])
        keys, vals = tokens(k_in[half]), tokens(v_in[half])
        for h in range(heads):
            cols = slice(h * HD, (h + 1) * HD)
            q, k, v = queries[:, cols], keys[:, cols], vals[:, cols]
            acc[half, :block, cols] = weighted(q[:block], k[:block], v[:block], True)
            acc[half, block:, cols] = weighted(q[block:], k[block:], v[block:], True) + weighted(
                q[block:], k[:block], v[:block], False
            )

    def finish(half):
        wait(p_in.at[half], r3_r.at[half])
        queries = tokens(q_in[half])
        for h in range(heads):
            cols = slice(h * HD, (h + 1) * HD)
            inter = jnp.dot(queries[:, cols], p_in[half, cols, :], preferred_element_type=F32)
            o_buf[half, :, :, cols] = (acc[half, :, cols] + inter).astype(BF16).reshape(nx, rows, HD)

        def o_copy(t, half):
            return o_buf.at[half, t], attn.at[:, columns(x, half)], o_s.at[half], o_r.at[half]

        spread_x(o_copy, half, False)

    for half in range(2):
        state(half)
        plane_sum(half)
        prefixes(half)
    for half in range(2):
        intra(half)
        finish(half)

    squares = jnp.zeros((rows, width), F32)
    for half in range(2):
        wait(attn.at[:, pl.ds(0, nx * width)], o_r.at[half])
        for t in range(nx):
            wide = attn[:, (2 * t + half) * width : (2 * t + half + 1) * width].astype(F32)
            squares = squares + wide * wide
    mean_square = jnp.sum(squares, axis=-1, keepdims=True) / attn.shape[1]
    scale[...] = lax.rsqrt(mean_square + 1e-05)

    for half in range(2):
        wait(v_in.at[half, pl.ds(0, nx - 1)], v_s.at[half])
        wait(k_in.at[half, pl.ds(0, nx - 1)], k_s.at[half])
        wait(q_in.at[half, pl.ds(0, nx - 1)], q_s.at[half])
        wait(o_buf.at[half, pl.ds(0, nx - 1)], o_s.at[half])
        wait(r1.at[half, pl.ds(0, GROUP - 1)], r1_s.at[half])
        wait(p_out.at[half, pl.ds(0, GROUP - 1)], r3_s.at[half])
        for i in range(1, nz):
            @pl.when(i > z)
            def _():
                wait(r_sum.at[half], r2_s.at[half, i])


def solution(mesh):
    nx, nz = mesh.shape["head"], mesh.shape["seq"] // GROUP

    def local(queries, keys_in, values_in, gain):
        rows, d = queries.shape
        width = d // nx // 2
        piece = width // GROUP
        vmem, pair = pltpu.VMEM, pltpu.SemaphoreType.DMA((2,))
        attn, scale = pl.pallas_call(
            functools.partial(kernel, nx, nz),
            out_shape=(jax.ShapeDtypeStruct((rows, d), BF16), jax.ShapeDtypeStruct((rows, 1), F32)),
            in_specs=[pl.BlockSpec(memory_space=pltpu.HBM)] * 3,
            out_specs=(pl.BlockSpec(memory_space=pltpu.VMEM),) * 2,
            scratch_shapes=[
                vmem((rows, d), BF16),
                vmem((rows, d), BF16),
                vmem((rows, d), BF16),
                vmem((rows, d), BF16),
                vmem((2, nx, rows, width), BF16),
                vmem((2, nx, rows, width), BF16),
                vmem((2, nx, rows, width), BF16),
                vmem((2, width, HD), F32),
                vmem((2, GROUP, piece, HD), F32),
                vmem((2, piece, HD), F32),
                vmem((2, nz, piece, HD), F32),
                vmem((2, piece, HD), F32),
                vmem((2, GROUP, piece, HD), BF16),
                vmem((2, width, HD), BF16),
                vmem((2, nx * rows, width), F32),
                vmem((2, nx, rows, width), BF16),
                pltpu.SemaphoreType.DMA((2,)),
            ]
            + [pair] * 8
            + [pltpu.SemaphoreType.DMA((2, nz))] * 2
            + [pair] * 4
            + [pltpu.SemaphoreType.REGULAR] * 2,
            compiler_params=pltpu.CompilerParams(
                collective_id=0, has_side_effects=True, vmem_limit_bytes=55836672
            ),
        )(queries, keys_in, values_in)
        return (attn.astype(F32) * scale * gain[None, :]).astype(BF16)

    placed = P(("seq", "head"), None)
    return jax.shard_map(
        local, mesh=mesh, in_specs=(placed, placed, placed, P()), out_specs=placed, check_vma=False
    )
```

```python
import functools

import jax
import jax.numpy as jnp
from jax import lax
from jax.experimental import pallas as pl
from jax.experimental.pallas import tpu as pltpu
from jax.sharding import PartitionSpec as P

HD = 128
GROUP = 16
MESH = pl.DeviceIdType.MESH
BF16, F32 = jnp.bfloat16, jnp.float32


def silu(x):
    wide = x.astype(F32)
    return (wide / (1.0 + jnp.exp(-wide))).astype(BF16)


def far_first(n):
    return sorted(range(1, n), key=lambda d: -min(d, n - d))


def kernel(nx, nz, q_hbm, k_hbm, v_hbm, attn, scale, q_raw, k_raw, k_act, q_act, v_in, k_in, q_in, t_buf, r1, r_sum, r2,
           below, p_out, p_in, acc, o_buf, in_sem, v_s, v_r, k_s, k_r, q_s, q_r, r1_s, r1_r, r2_s, r2_r, r3_s, r3_r, o_s, o_r,
           late, above):
    x, s = lax.axis_index("head"), lax.axis_index("seq")
    g, z = lax.rem(s, GROUP), s // GROUP
    rows = q_raw.shape[0]
    width = k_in.shape[-1]
    heads = width // HD
    toks = nx * rows
    piece = t_buf.shape[1] // GROUP

    def at_x(t):
        return {"head": t}

    def at_g(t):
        return {"seq": z * GROUP + t}

    def at_z(t):
        return {"seq": t * GROUP + g}

    first = (x == 0) & (s == 0)
    line_first = (s == 0) & (x != 0)
    plane_first = (x == 0) & (z == 0) & (g != 0)
    stack_first = (x == 0) & (g == 0) & (z != 0)

    loads = [
        pltpu.make_async_copy(k_hbm, k_raw, in_sem.at[0]),
        pltpu.make_async_copy(q_hbm, q_raw, in_sem.at[1]),
    ]
    for load in loads:
        load.start()

    barrier = pltpu.get_barrier_semaphore()
    peers = ((nx, x, at_x), (GROUP, g, at_g))

    def greet(sem):
        for n, me, at in peers:
            for d in range(1, n):
                pl.semaphore_signal(sem, inc=1, device_id=at(lax.rem(me + d, n)), device_id_type=MESH)

    @pl.when(jnp.logical_not(first))
    def _():
        greet(barrier)

    for i in range(nz):
        @pl.when((i > z) & jnp.logical_not(first) | (i == 0) & stack_first)
        def _():
            pl.semaphore_signal(barrier, inc=1, device_id=at_z(i), device_id_type=MESH)

    stack_below = jnp.where(first, nz - 1, z - stack_first.astype(jnp.int32))
    pl.semaphore_wait(barrier, nx + GROUP - 2 + stack_below - (line_first | plane_first).astype(jnp.int32))

    @pl.when(first)
    def _():
        greet(late)

    for i in range(nz - 1):
        @pl.when((i < z) & jnp.logical_not(stack_first & (i == 0)))
        def _():
            pl.semaphore_signal(above, inc=1, device_id=at_z(i), device_id_type=MESH)

    def columns(t, half):
        return pl.ds(pl.multiple_of(t * 2 * width + half * width, width), width)

    def v_copy(t, half):
        return v_hbm.at[:, columns(t, half)], v_in.at[half, x], v_s.at[half], v_r.at[half]

    def k_copy(t, half):
        return k_act.at[:, columns(t, half)], k_in.at[half, x], k_s.at[half], k_r.at[half]

    def q_copy(t, half):
        return q_act.at[:, columns(t, half)], q_in.at[half, x], q_s.at[half], q_r.at[half]

    def activate(raw, act, half):
        for t in range(nx):
            cols = slice((2 * t + half) * width, (2 * t + half + 1) * width)
            act[:, cols] = silu(raw[:, cols])

    def remote(copy, device):
        src, dst, send, recv = copy
        pltpu.make_async_remote_copy(src, dst, send, recv, device_id=device, device_id_type=MESH).start()

    def local(copy):
        src, dst, _, recv = copy
        pltpu.make_async_copy(src, dst, recv).start()

    def wait(ref, sem):
        pltpu.make_async_copy(ref, ref, sem).wait()

    def spread_x(copy_of, half, open_late):
        for d in far_first(nx):
            t = lax.rem(x + d, nx)
            if open_late:
                @pl.when(jnp.logical_not((s == 0) & (t == 0)))
                def _():
                    remote(copy_of(t, half), at_x(t))
            else:
                remote(copy_of(t, half), at_x(t))
        local(copy_of(x, half))

    spread_x(v_copy, 0, True)
    loads[0].wait()
    activate(k_raw, k_act, 0)
    spread_x(k_copy, 0, True)
    activate(k_raw, k_act, 1)

    @pl.when(line_first | plane_first)
    def _():
        pl.semaphore_wait(late, 1)

    @pl.when(line_first)
    def _():
        remote(v_copy(0, 0), at_x(0))
        remote(k_copy(0, 0), at_x(0))

    spread_x(v_copy, 1, False)
    spread_x(k_copy, 1, False)
    loads[1].wait()
    for half in range(2):
        activate(q_raw, q_act, half)
        spread_x(q_copy, half, False)

    def tokens(ref):
        return ref.reshape(toks, width)

    def state(half):
        wait(v_in.at[half], v_r.at[half])
        wait(k_in.at[half], k_r.at[half])
        keys, vals = tokens(k_in[half]), tokens(v_in[half])
        for h in range(heads):
            cols = slice(h * HD, (h + 1) * HD)
            t_buf[half, cols, :] = lax.dot_general(
                keys[:, cols], vals[:, cols], (((0,), (0,)), ((), ())), preferred_element_type=F32
            )
        for d in range(GROUP):
            t = lax.rem(g + d, GROUP) if d else g
            span = pl.ds(pl.multiple_of(t * piece, piece), piece)
            copy = (t_buf.at[half, span], r1.at[half, g], r1_s.at[half], r1_r.at[half])
            if d:
                remote(copy, at_g(t))
            else:
                local(copy)

    def plane_sum(half):
        wait(r1.at[half], r1_r.at[half])
        r_sum[half] = jnp.sum(r1[half], axis=0)
        if half == 0:
            @pl.when((z < nz - 1) & jnp.logical_not(first))
            def _():
                pl.semaphore_wait(above, nz - 1 - z)

        for i in range(1, nz):
            @pl.when(i > z)
            def _():
                remote((r_sum.at[half], r2.at[half, z], r2_s.at[half, i], r2_r.at[half, z]), at_z(i))

    def prefixes(half):
        below[half] = jnp.zeros(r_sum.shape[1:], F32)
        for i in range(nz - 1):
            @pl.when(i < z)
            def _():
                wait(r2.at[half, i], r2_r.at[half, i])
                below[half] += r2[half, i]
        running = below[half]
        for j in range(GROUP):
            p_out[half, j] = running.astype(BF16)
            running = running + r1[half, j]
        for d in range(GROUP):
            t = lax.rem(g + d, GROUP) if d else g
            span = pl.ds(pl.multiple_of(g * piece, piece), piece)
            copy = (p_out.at[half, t], p_in.at[half, span], r3_s.at[half], r3_r.at[half])
            if d:
                remote(copy, at_g(t))
            else:
                local(copy)

    block = toks // 2
    causal = lax.broadcasted_iota(jnp.int32, (block, block), 1) <= lax.broadcasted_iota(jnp.int32, (block, block), 0)

    def weighted(queries, keys, vals, masked):
        scores = lax.dot_general(queries, keys, (((1,), (1,)), ((), ())), preferred_element_type=F32)
        if masked:
            scores = jnp.where(causal, scores, 0.0)
        return jnp.dot(scores.astype(BF16), vals, preferred_element_type=F32)

    def intra(half):
        wait(q_in.at[half], q_r.at[half])
        queries = tokens(q_in[half])
        keys, vals = tokens(k_in[half]), tokens(v_in[half])
        for h in range(heads):
            cols = slice(h * HD, (h + 1) * HD)
            q, k, v = queries[:, cols], keys[:, cols], vals[:, cols]
            acc[half, :block, cols] = weighted(q[:block], k[:block], v[:block], True)
            acc[half, block:, cols] = weighted(q[block:], k[block:], v[block:], True) + weighted(
                q[block:], k[:block], v[:block], False
            )

    def finish(half):
        wait(p_in.at[half], r3_r.at[half])
        queries = tokens(q_in[half])
        for h in range(heads):
            cols = slice(h * HD, (h + 1) * HD)
            inter = jnp.dot(queries[:, cols], p_in[half, cols, :], preferred_element_type=F32)
            o_buf[half, :, :, cols] = (acc[half, :, cols] + inter).astype(BF16).reshape(nx, rows, HD)

        def o_copy(t, half):
            return o_buf.at[half, t], attn.at[:, columns(x, half)], o_s.at[half], o_r.at[half]

        spread_x(o_copy, half, False)

    for half in range(2):
        state(half)
        plane_sum(half)
        prefixes(half)
    for half in range(2):
        intra(half)
        finish(half)

    squares = jnp.zeros((rows, width), F32)
    for half in range(2):
        wait(attn.at[:, pl.ds(0, nx * width)], o_r.at[half])
        for t in range(nx):
            wide = attn[:, (2 * t + half) * width : (2 * t + half + 1) * width].astype(F32)
            squares = squares + wide * wide
    mean_square = jnp.sum(squares, axis=-1, keepdims=True) / attn.shape[1]
    scale[...] = lax.rsqrt(mean_square + 1e-05)

    for half in range(2):
        wait(v_in.at[half, pl.ds(0, nx - 1)], v_s.at[half])
        wait(k_in.at[half, pl.ds(0, nx - 1)], k_s.at[half])
        wait(q_in.at[half, pl.ds(0, nx - 1)], q_s.at[half])
        wait(o_buf.at[half, pl.ds(0, nx - 1)], o_s.at[half])
        wait(r1.at[half, pl.ds(0, GROUP - 1)], r1_s.at[half])
        wait(p_out.at[half, pl.ds(0, GROUP - 1)], r3_s.at[half])
        for i in range(1, nz):
            @pl.when(i > z)
            def _():
                wait(r_sum.at[half], r2_s.at[half, i])


def solution(mesh):
    nx, nz = mesh.shape["head"], mesh.shape["seq"] // GROUP

    def local(queries, keys_in, values_in, gain):
        rows, d = queries.shape
        width = d // nx // 2
        piece = width // GROUP
        vmem, pair = pltpu.VMEM, pltpu.SemaphoreType.DMA((2,))
        attn, scale = pl.pallas_call(
            functools.partial(kernel, nx, nz),
            out_shape=(jax.ShapeDtypeStruct((rows, d), BF16), jax.ShapeDtypeStruct((rows, 1), F32)),
            in_specs=[pl.BlockSpec(memory_space=pltpu.HBM)] * 3,
            out_specs=(pl.BlockSpec(memory_space=pltpu.VMEM),) * 2,
            scratch_shapes=[
                vmem((rows, d), BF16),
                vmem((rows, d), BF16),
                vmem((rows, d), BF16),
                vmem((rows, d), BF16),
                vmem((2, nx, rows, width), BF16),
                vmem((2, nx, rows, width), BF16),
                vmem((2, nx, rows, width), BF16),
                vmem((2, width, HD), F32),
                vmem((2, GROUP, piece, HD), F32),
                vmem((2, piece, HD), F32),
                vmem((2, nz, piece, HD), F32),
                vmem((2, piece, HD), F32),
                vmem((2, GROUP, piece, HD), BF16),
                vmem((2, width, HD), BF16),
                vmem((2, nx * rows, width), F32),
                vmem((2, nx, rows, width), BF16),
                pltpu.SemaphoreType.DMA((2,)),
            ]
            + [pair] * 8
            + [pltpu.SemaphoreType.DMA((2, nz))] * 2
            + [pair] * 4
            + [pltpu.SemaphoreType.REGULAR] * 2,
            compiler_params=pltpu.CompilerParams(
                collective_id=0, has_side_effects=True, vmem_limit_bytes=55836672
            ),
        )(queries, keys_in, values_in)
        return (attn.astype(F32) * scale * gain[None, :]).astype(BF16)

    placed = P(("seq", "head"), None)
    return jax.shard_map(
        local, mesh=mesh, in_specs=(placed, placed, placed, P()), out_specs=placed, check_vma=False
    )
```
